32 devices in a mesh: rows: 8 (over y, x, core), tiles: 4 (over z).
Axes of the slice: x: 2, y: 2, z: 4, core: 2. Of those that a mesh axis runs over, the one named last changes fastest.
Arguments:
- response_tiles: bfloat16 [8, 4, 15, 2, 256, 256], P('rows', 'tiles'), as said below
- tile_rows: int32 [8, 4, 15], P('rows', 'tiles'), may hold values from 0 to 2, as said below
- tile_cols: int32 [8, 4, 15], P('rows', 'tiles'), may hold values from 0 to 23, as said below
- tile_counts: int32 [8, 4], P('rows', 'tiles'), may hold values from 2 to 15, as said below
- start_block: bfloat16 [6144, 256], P(('rows', 'tiles')), may hold values from -6 to 6
Outputs:
- subspace: float32 [6144, 256], P(('rows', 'tiles'))
- rayleigh: float32 [2, 128, 128], replicated
The draws below stay inside these ranges and needn't reach their ends.
Inputs may be any that keep to these rules, and one draw needn't show every extreme that they name: `tile_rows`: block rows within the group; every list's first two slots are live. `tile_cols`: A slot of group g at block row g * 3 + r has its column block within 3 of that block row, cut to the grid; in every list slot 0 lies 3 blocks below the row (or at column block 0) and slot 1 lies 3 blocks above it (or at the last column block). `tile_counts`: some tile list is full in every draw. `response_tiles`: real tiles of full rank; dead slots hold finite values.
All inputs are finite; a program needn't handle non-finite values.
Results may differ from the reference program's by a relative error of at most 0.0038.
Values may be sent and summed in bfloat16 or wider, within the bound.
A program may use at most 64 MiB of HBM per device.

```python
import math
import jax
import jax.numpy as jnp
import numpy as np
from jax import lax

TILE = 256
COLS = 128
RB = 3
ITERS = 2
ROW_GROUPS = 8
TILE_GROUPS = 4
NT = 15
NB = 24
NODES = 6144


def pattern_pair(key):
    pattern_key = jax.random.fold_in(key, 7)
    keys = jax.random.split(pattern_key, 2)
    extent = (ROW_GROUPS, TILE_GROUPS, NT)
    local_rows = jax.random.randint(keys[0], extent, 0, RB)
    reaches = jax.random.randint(keys[1], extent, -RB, RB + 1)
    reaches = reaches.at[:, :, 0].set(-RB).at[:, :, 1].set(RB)
    global_rows = jnp.arange(ROW_GROUPS, dtype=jnp.int32)[:, None, None] * RB + local_rows
    columns = jnp.clip(global_rows + reaches, 0, NB - 1)
    return (local_rows.astype(jnp.int32), columns.astype(jnp.int32))


def draw_tile_rows(key, part):
    return pattern_pair(key)[0]


def draw_tile_cols(key, part):
    return pattern_pair(key)[1]


def draw_tile_counts(key, part):
    keys = jax.random.split(jax.random.fold_in(key, 13), 3)
    extent = (ROW_GROUPS, TILE_GROUPS)
    first_draw = jax.random.randint(keys[0], extent, 0, NT + 1)
    second_draw = jax.random.randint(keys[1], extent, 0, NT + 1)
    counts = jnp.maximum(first_draw * second_draw // NT, 2)
    chosen = jax.random.randint(keys[2], (), 0, ROW_GROUPS * TILE_GROUPS)
    counts = counts.reshape(-1).at[chosen].set(NT).reshape(extent)
    return counts.astype(jnp.int32)


def draw_response_tiles(key, part):
    keys = jax.random.split(jax.random.fold_in(key, 29), 3)
    extent = (ROW_GROUPS, TILE_GROUPS, NT, 2, TILE, TILE)
    spread_scale = 1.0 / math.sqrt(16.0 * TILE)
    entries = jax.random.normal(keys[0], extent, jnp.float32)
    upper_scale = 1.7
    row_scale = jnp.exp(jax.random.uniform(keys[1], (ROW_GROUPS, TILE_GROUPS, NT, 1, TILE, 1), jnp.float32, 0.0, math.log(upper_scale)))
    col_scale = jnp.exp(jax.random.uniform(keys[2], (ROW_GROUPS, TILE_GROUPS, NT, 1, 1, TILE), jnp.float32, 0.0, math.log(upper_scale)))
    rising = 3.0 ** (jnp.arange(ROW_GROUPS, dtype=jnp.float32) / max(ROW_GROUPS - 1, 1))
    rising = rising.reshape(ROW_GROUPS, 1, 1, 1, 1, 1)
    return (entries * spread_scale * row_scale * col_scale * rising).astype(jnp.bfloat16)


def levels(key, shape, shards, least, largest):
    def one(axis_at, blocks):
        heights = jax.random.uniform(jax.random.fold_in(jax.random.fold_in(key, 6), axis_at), (blocks,), jnp.float32, least / len(shards), largest / len(shards))
        return jnp.repeat(jnp.exp(heights), shape[axis_at] // blocks).reshape((-1,) + (1,) * (len(shape) - axis_at - 1))

    loudness = one(*shards[0])
    for cut in shards[1:]:
        loudness = loudness * one(*cut)
    return loudness


def bell_draw(rng, shape, scale, most, pieces=(), held_as=jnp.bfloat16):
    factor_of = levels(rng, shape, pieces, -0.22, 0.18) if pieces else 1.0
    values = jax.random.normal(rng, shape, jnp.float32) * scale * factor_of
    return jnp.minimum(jnp.maximum(values, -most), most).astype(held_as)


def setup_inputs(seed: int = 0) -> dict:
    key_list = jax.random.split(jax.random.key(seed), 6)
    response_tiles = draw_response_tiles(jax.random.fold_in(key_list[5], 71), 0)
    tile_rows = draw_tile_rows(jax.random.fold_in(key_list[5], 71), 0)
    tile_cols = draw_tile_cols(jax.random.fold_in(key_list[5], 71), 0)
    tile_counts = draw_tile_counts(jax.random.fold_in(key_list[5], 71), 0)
    start_block = bell_draw(key_list[4], (NODES, 2 * COLS), 1.0, 6.0, ((0, 32),))
    return {"response_tiles": response_tiles, "tile_rows": tile_rows, "tile_cols": tile_cols, "tile_counts": tile_counts, "start_block": start_block}


HIGH = lax.Precision.HIGHEST

def inner(left_side, right_side):
    return lax.dot_general(left_side, right_side, (((0,), (0,)), ((), ())), precision=HIGH)

def whitening(gram, columns, nodes):
    upper_left = gram[:columns, :columns]
    upper_right = gram[:columns, columns:]
    lower_left = gram[columns:, :columns]
    lower_right = gram[columns:, columns:]
    real_gram = upper_left + lower_right
    imag_gram = upper_right - lower_left
    embedded = jnp.concatenate([jnp.concatenate([real_gram, imag_gram], 1), jnp.concatenate([-imag_gram, real_gram], 1)], 0)
    pairing = np.stack([np.arange(columns), np.arange(columns) + columns], 1).reshape(-1)
    unpairing = np.argsort(pairing)
    paired = embedded[pairing][:, pairing]
    factor = jnp.linalg.cholesky(paired)
    identity = jnp.eye(2 * columns, dtype=gram.dtype)
    inverse = jax.scipy.linalg.solve_triangular(factor, identity, lower=True)
    return inverse.T[unpairing][:, unpairing] * math.sqrt(nodes)

def rayleigh_of(products, columns, nodes):
    real_part = products[:columns, :columns] + products[columns:, columns:]
    imag_part = products[:columns, columns:] - products[columns:, :columns]
    return jnp.stack([real_part, imag_part]) / nodes

def forward(flat_tiles, global_rows, flat_cols, live_mask, narrow, tile_size):
    width = narrow.shape[1]
    half = width // 2

    def visit(slot_index, totals):
        pair = flat_tiles[slot_index].astype(jnp.float32)
        source = lax.dynamic_slice_in_dim(narrow, flat_cols[slot_index] * tile_size, tile_size, 0).astype(jnp.float32)
        real_term = jnp.dot(pair[0], source, precision=HIGH)
        imag_term = jnp.dot(pair[1], source, precision=HIGH)
        term = jnp.concatenate([real_term[:, :half] - imag_term[:, half:], real_term[:, half:] + imag_term[:, :half]], 1)
        term = term * live_mask[slot_index]
        target = global_rows[slot_index] * tile_size
        present = lax.dynamic_slice_in_dim(totals, target, tile_size, 0)
        return lax.dynamic_update_slice_in_dim(totals, present + term, target, 0)
    return lax.fori_loop(0, flat_cols.shape[0], visit, jnp.zeros(narrow.shape, jnp.float32))

def adjoint(flat_tiles, global_rows, flat_cols, live_mask, narrow, tile_size):
    width = narrow.shape[1]
    half = width // 2

    def visit(slot_index, totals):
        pair = flat_tiles[slot_index].astype(jnp.float32)
        source = lax.dynamic_slice_in_dim(narrow, global_rows[slot_index] * tile_size, tile_size, 0).astype(jnp.float32)
        real_term = inner(pair[0], source)
        imag_term = inner(pair[1], source)
        term = jnp.concatenate([real_term[:, :half] + imag_term[:, half:], real_term[:, half:] - imag_term[:, :half]], 1)
        term = term * live_mask[slot_index]
        target = flat_cols[slot_index] * tile_size
        present = lax.dynamic_slice_in_dim(totals, target, tile_size, 0)
        return lax.dynamic_update_slice_in_dim(totals, present + term, target, 0)
    return lax.fori_loop(0, flat_cols.shape[0], visit, jnp.zeros(narrow.shape, jnp.float32))

def reference(response_tiles, tile_rows, tile_cols, tile_counts, start_block):
    groups = tile_rows.shape[0]
    slot_count = tile_rows.shape[2]
    tile_size = response_tiles.shape[-1]
    flat_tiles = response_tiles.reshape(-1, 2, tile_size, tile_size)
    offsets = (jnp.arange(groups, dtype=jnp.int32) * RB).astype(jnp.int32)
    global_rows = (tile_rows + offsets[:, None, None]).reshape(-1).astype(jnp.int32)
    flat_cols = tile_cols.reshape(-1).astype(jnp.int32)
    live_mask = (jnp.arange(slot_count, dtype=jnp.int32)[None, None, :] < tile_counts[:, :, None]).astype(jnp.float32).reshape(-1)
    nodes = start_block.shape[0]
    columns = start_block.shape[1] // 2
    current = start_block.astype(jnp.float32)
    rayleigh = jnp.zeros((2, columns, columns), jnp.float32)
    for iteration in range(ITERS):
        narrow = current.astype(jnp.bfloat16)
        response = forward(flat_tiles, global_rows, flat_cols, live_mask, narrow, tile_size)
        response_narrow = response.astype(jnp.bfloat16)
        image = adjoint(flat_tiles, global_rows, flat_cols, live_mask, response_narrow, tile_size) + current
        gram = inner(image, image)
        if iteration == ITERS - 1:
            rayleigh = rayleigh_of(inner(current, image), columns, nodes)
        current = jnp.dot(image, whitening(gram, columns, nodes), precision=HIGH)
    return (current, rayleigh)
```

```python
import functools
import math

import jax
import jax.numpy as jnp
from jax import lax
from jax.experimental import pallas as pl
from jax.experimental.pallas import tpu as pltpu
from jax.sharding import PartitionSpec as P

HIGH = lax.Precision.HIGHEST
MESH = pl.DeviceIdType.MESH
VMEM_BYTES = 48 * 1024 * 1024
F32 = jnp.float32
BF16 = jnp.bfloat16


def ordered(key, other, outs):
    count = key.shape[0]
    slot = jnp.arange(count, dtype=jnp.int32)
    before = (key[:, None] < key[None, :]) | (
        (key[:, None] == key[None, :]) & (slot[:, None] < slot[None, :])
    )
    rank = jnp.sum(before.astype(jnp.int32), 0)
    hot = (rank[:, None] == slot[None, :]).astype(jnp.int32)
    order = jnp.sum(hot * slot[:, None], 0)
    target = jnp.sum(hot * key[:, None], 0)
    source = jnp.sum(hot * other[:, None], 0)
    same = jnp.concatenate([jnp.zeros((1,), bool), target[1:] == target[:-1]])
    previous = jnp.where(same, slot, 0)
    out = jnp.arange(outs, dtype=jnp.int32)
    upto = jnp.sum((target[:, None] <= out[None, :]).astype(jnp.int32), 0)
    present = jnp.any(target[:, None] == out[None, :], 0)
    return jnp.concatenate([order, source, previous, jnp.where(present, upto, 0)])


def step_kernel(
    n_g, n_t, with_products, slots_n, blocks,
    plan, tiles, current, image_out, gram_out,
    turned, ext, ext_blocks, z_blocks, runs, part32, part, rs_in, z_rows, spread, mid, halo_in, ar_out, ar_in,
    gram_mine, gram_in, gram_rows, gram_sum,
    gz_s, gz_r, gh_s, gh_r, rs_s, rs_r, ag_s, ag_r, ah_s, ah_r, ar_s, ar_r,
    g1_s, g1_r, g2_s, g2_r, g3_s, g3_r,
):
    g = lax.axis_index("rows")
    t = lax.axis_index("tiles")
    has_low = g > 0
    has_high = g < n_g - 1
    tile = tiles.shape[-1]
    shard, width = current.shape
    half = width // 2
    own = shard * n_t

    barrier = pltpu.get_barrier_semaphore()
    for k in range(1, n_t):
        pl.semaphore_signal(barrier, inc=1, device_id=(g, (t + k) % n_t), device_id_type=MESH)

    for k in range(1, n_g):
        pl.semaphore_signal(barrier, inc=1, device_id=((g + k) % n_g, t), device_id_type=MESH)
    pl.semaphore_wait(barrier, n_t + n_g - 2)

    def remote(src, dst, send, recv, dev):
        return pltpu.make_async_remote_copy(
            src_ref=src, dst_ref=dst, send_sem=send, recv_sem=recv,
            device_id=dev, device_id_type=MESH,
        )

    def shard_at(base, index):
        return pl.ds(pl.multiple_of(base + index * shard, 64), shard)

    def gather_z(k):
        at = ext.at[shard_at(own, t)]
        return remote(at, at, gz_s.at[k], gz_r.at[k], (g, (t + k) % n_t))

    def landed_z(k):
        at = ext.at[shard_at(own, (t - k + n_t) % n_t)]
        return remote(at, at, gz_s.at[k], gz_r.at[k], (g, (t + k) % n_t))

    def halo(k, up):
        index = (t - k + n_t) % n_t
        src = ext.at[shard_at(own, index)]
        if up:
            return remote(src, ext.at[shard_at(0, index)], gh_s.at[0, k], gh_r.at[0, k], (g + 1, t))
        return remote(src, ext.at[shard_at(2 * own, index)], gh_s.at[1, k], gh_r.at[1, k], (g - 1, t))

    def landed_halo(k, low):
        index = (t - k + n_t) % n_t
        if low:
            at = ext.at[shard_at(0, index)]
            return remote(at, at, gh_s.at[0, k], gh_r.at[0, k], (g - 1, t))
        at = ext.at[shard_at(2 * own, index)]
        return remote(at, at, gh_s.at[1, k], gh_r.at[1, k], (g + 1, t))

    def both(do_up, do_down):
        pl.when(has_high)(do_up)
        pl.when(has_low)(do_down)

    ext[shard_at(own, t), :] = current[...].astype(BF16)
    for k in range(1, n_t):
        gather_z(k).start()
    both(lambda: halo(0, True).start(), lambda: halo(0, False).start())

    @pl.when(jnp.logical_not(has_low))
    def _():
        ext[0:own, :] = jnp.zeros((own, width), BF16)
        halo_in[0] = jnp.zeros((own, width), BF16)

    @pl.when(jnp.logical_not(has_high))
    def _():
        ext[2 * own : 3 * own, :] = jnp.zeros((own, width), BF16)
        halo_in[1] = jnp.zeros((own, width), BF16)

    runs[0] = jnp.zeros((tile, width), F32)
    for k in range(1, n_t):
        landed_z(k).wait_recv()
        both(lambda k=k: halo(k, True).start(), lambda k=k: halo(k, False).start())

    def turn(s, _):
        for c in range(2):
            turned[s, pl.ds(c * tile, tile), :] = tiles[s, c].T
        return 0

    lax.fori_loop(0, slots_n, turn, 0)
    for k in range(n_t):
        both(lambda k=k: landed_halo(k, False).wait_recv(), lambda k=k: landed_halo(k, True).wait_recv())

    for c in range(3 * blocks):
        ext_blocks[c] = ext[pl.ds(c * tile, tile), :]

    def forward(s, _):
        order = plan[s]
        source = ext_blocks[plan[slots_n + s]]
        pair = tiles[order].reshape(2 * tile, tile)
        both_terms = jnp.dot(pair, source, preferred_element_type=F32)
        re, im = both_terms[:tile], both_terms[tile:]
        term = jnp.concatenate(
            [re[:, :half] - im[:, half:], re[:, half:] + im[:, :half]], 1
        )
        runs[s + 1] = term + runs[plan[2 * slots_n + s]]
        return 0

    lax.fori_loop(0, slots_n, forward, 0)
    for r in range(blocks):
        block = runs[plan[3 * slots_n + r]]
        part32[pl.ds(r * tile, tile), :] = block
        part[pl.ds(r * tile, tile), :] = block.astype(BF16)

    def reduce_z(k):
        dest = (t + k) % n_t
        return remote(part.at[shard_at(0, dest)], rs_in.at[k], rs_s.at[k], rs_r.at[k], (g, dest))

    for k in range(1, n_t):
        reduce_z(k).start()
    total = part32[shard_at(0, t), :]
    for k in range(1, n_t):
        reduce_z(k).wait_recv()
        total += rs_in[k].astype(F32)
    z_rows[shard_at(0, t), :] = total.astype(BF16)

    def spread_z(k, landed):
        at = z_rows.at[shard_at(0, (t - k + n_t) % n_t if landed else t)]
        return remote(at, at, ag_s.at[k], ag_r.at[k], (g, (t + k) % n_t))

    for k in range(1, n_t):
        spread_z(k, False).start()
    for k in range(1, n_t):
        spread_z(k, True).wait_recv()

    for r in range(blocks):
        z_blocks[r] = z_rows[pl.ds(r * tile, tile), :]

    base = 3 * slots_n + blocks

    def adjoint(s, _):
        order = plan[base + s]
        source = z_blocks[plan[base + slots_n + s]]
        both_terms = jnp.dot(turned[order], source, preferred_element_type=F32)
        re, im = both_terms[:tile], both_terms[tile:]
        term = jnp.concatenate(
            [re[:, :half] + im[:, half:], re[:, half:] - im[:, :half]], 1
        )
        runs[s + 1] = term + runs[plan[base + 2 * slots_n + s]]
        return 0

    lax.fori_loop(0, slots_n, adjoint, 0)
    for c in list(range(blocks)) + list(range(2 * blocks, 3 * blocks)):
        spread[pl.ds(c * tile, tile), :] = runs[plan[base + 3 * slots_n + c]].astype(BF16)

    def rim(k, up):
        dest = (t + k) % n_t
        src = spread.at[shard_at(2 * own if up else 0, dest)]
        side = 0 if up else 1
        return remote(
            src, halo_in.at[side, shard_at(0, dest)], ah_s.at[side, k], ah_r.at[side, k],
            (g + 1 if up else g - 1, t),
        )

    for k in list(range(1, n_t)) + [0]:
        both(lambda k=k: rim(k, True).start(), lambda k=k: rim(k, False).start())
    for c in range(blocks):
        mid[pl.ds(c * tile, tile), :] = runs[plan[base + 3 * slots_n + blocks + c]]

    def sum_to(k):
        dest = (t + k) % n_t
        return remote(ar_out.at[k], ar_in.at[k], ar_s.at[k], ar_r.at[k], (g, dest))

    for k in list(range(1, n_t)) + [0]:
        both(lambda k=k: rim(k, False).wait_recv(), lambda k=k: rim(k, True).wait_recv())
        at = shard_at(0, (t + k) % n_t)
        total = mid[at, :] + halo_in[0, at, :].astype(F32) + halo_in[1, at, :].astype(F32)
        if k:
            ar_out[k] = total.astype(BF16)
            sum_to(k).start()
    for k in range(1, n_t):
        sum_to(k).wait_recv()
        total += ar_in[k].astype(F32)
    image = total + current[...]
    image_out[...] = image

    def cross(left, right):
        return lax.dot_general(
            left, right, (((0,), (0,)), ((), ())), precision=HIGH, preferred_element_type=F32
        )

    full = cross(image, image)
    gram_mine[0:half, :] = jnp.concatenate(
        [full[:half, :half] + full[half:, half:], full[:half, half:] - full[half:, :half]], 1
    )
    if with_products:
        full = cross(current[...], image)
        gram_mine[half : 2 * half, :] = jnp.concatenate(
            [full[:half, :half] + full[half:, half:], full[:half, half:] - full[half:, :half]], 1
        )
    piece = gram_mine.shape[0] // n_t

    def piece_at(index):
        return pl.ds(pl.multiple_of(index * piece, 8), piece)

    def gram_one(k):
        dest = (t + k) % n_t
        return remote(gram_mine.at[piece_at(dest)], gram_in.at[k], g1_s.at[k], g1_r.at[k], (g, dest))

    for k in range(1, n_t):
        gram_one(k).start()
    total = gram_mine[piece_at(t), :]
    for k in range(1, n_t):
        gram_one(k).wait_recv()
        total += gram_in[k]
    gram_rows[g] = total

    def gram_two(k, landed):
        at = gram_rows.at[(g - k + n_g) % n_g if landed else g]
        return remote(at, at, g2_s.at[k], g2_r.at[k], ((g + k) % n_g, t))

    for k in range(1, n_g):
        gram_two(k, False).start()
    for k in range(1, n_g):
        gram_two(k, True).wait_recv()
    total = gram_rows[0]
    for k in range(1, n_g):
        total += gram_rows[k]
    gram_sum[piece_at(t), :] = total

    def gram_three(k, landed):
        at = gram_sum.at[piece_at((t - k + n_t) % n_t if landed else t)]
        return remote(at, at, g3_s.at[k], g3_r.at[k], (g, (t + k) % n_t))

    for k in range(1, n_t):
        gram_three(k, False).start()
    for k in range(1, n_t):
        gram_three(k, True).wait_recv()
    gram_out[...] = gram_sum[...]

    for k in range(1, n_t):
        gather_z(k).wait_send()
        reduce_z(k).wait_send()
        spread_z(k, False).wait_send()
        sum_to(k).wait_send()
        gram_one(k).wait_send()
        gram_three(k, False).wait_send()
    for k in range(n_t):
        both(lambda k=k: halo(k, True).wait_send(), lambda k=k: halo(k, False).wait_send())
        both(lambda k=k: rim(k, True).wait_send(), lambda k=k: rim(k, False).wait_send())
    for k in range(1, n_g):
        gram_two(k, False).wait_send()


def step(plan, tiles, current, with_products):
    n_g, n_t = lax.axis_size("rows"), lax.axis_size("tiles")
    slots_n, _, tile, _ = tiles.shape
    shard, width = current.shape
    own = shard * n_t
    blocks = own // tile
    rows = width if with_products else width // 2
    dma = pltpu.SemaphoreType.DMA
    vmem = pl.BlockSpec(memory_space=pltpu.VMEM)
    return pl.pallas_call(
        functools.partial(step_kernel, n_g, n_t, with_products, slots_n, blocks),
        out_shape=(
            jax.ShapeDtypeStruct((shard, width), F32),
            jax.ShapeDtypeStruct((rows, width), F32),
        ),
        in_specs=[pl.BlockSpec(memory_space=pltpu.SMEM), vmem, vmem],
        out_specs=(vmem, vmem),
        scratch_shapes=[
            pltpu.VMEM((slots_n, 2 * tile, tile), BF16),
            pltpu.VMEM((3 * own, width), BF16),
            pltpu.VMEM((3 * blocks, tile, width), BF16),
            pltpu.VMEM((blocks, tile, width), BF16),
            pltpu.VMEM((slots_n + 1, tile, width), F32),
            pltpu.VMEM((own, width), F32),
            pltpu.VMEM((own, width), BF16),
            pltpu.VMEM((n_t, shard, width), BF16),
            pltpu.VMEM((own, width), BF16),
            pltpu.VMEM((3 * own, width), BF16),
            pltpu.VMEM((own, width), F32),
            pltpu.VMEM((2, own, width), BF16),
            pltpu.VMEM((n_t, shard, width), BF16),
            pltpu.VMEM((n_t, shard, width), BF16),
            pltpu.VMEM((rows, width), F32),
            pltpu.VMEM((n_t, rows // n_t, width), F32),
            pltpu.VMEM((n_g, rows // n_t, width), F32),
            pltpu.VMEM((rows, width), F32),
            dma((n_t,)), dma((n_t,)), dma((2, n_t)), dma((2, n_t)),
            dma((n_t,)), dma((n_t,)), dma((n_t,)), dma((n_t,)),
            dma((2, n_t)), dma((2, n_t)), dma((n_t,)), dma((n_t,)),
            dma((n_t,)), dma((n_t,)), dma((n_g,)), dma((n_g,)), dma((n_t,)), dma((n_t,)),
        ],
        compiler_params=pltpu.CompilerParams(
            collective_id=1 if with_products else 0,
            has_side_effects=True,
            vmem_limit_bytes=VMEM_BYTES,
        ),
    )(plan, tiles, current)


def whiten_kernel(nodes, gram, image, out, work_r, work_i):
    size = work_r.shape[0]
    work_r[...] = gram[0:size, 0:size]
    work_i[...] = -gram[0:size, size : 2 * size]
    lane = lax.broadcasted_iota(jnp.int32, (size, size), 1)
    sub = lax.broadcasted_iota(jnp.int32, (size, size), 0)
    lane_row = lax.broadcasted_iota(jnp.int32, (1, size), 1)
    sub_col = lax.broadcasted_iota(jnp.int32, (size, 1), 0)

    def eliminate(j, pivots):
        full_r, full_i = work_r[...], work_i[...]
        at = lane == j
        col_r = jnp.sum(jnp.where(at, full_r, 0.0), 1, keepdims=True)
        col_i = jnp.sum(jnp.where(at, full_i, 0.0), 1, keepdims=True)
        row_r = work_r[pl.ds(j, 1), :]
        row_i = work_i[pl.ds(j, 1), :]
        here = lane_row == j
        pivot = jnp.sum(jnp.where(here, row_r, 0.0), 1, keepdims=True)
        inverse = 1.0 / pivot
        below = sub_col > j
        fac_r = jnp.where(below, col_r * inverse, 0.0)
        fac_i = jnp.where(below, col_i * inverse, 0.0)
        row_r = jnp.where(here, 1.0, row_r)
        row_i = jnp.where(here, 0.0, row_i)
        work_r[...] = jnp.where(at, 0.0, full_r) - (fac_r * row_r - fac_i * row_i)
        work_i[...] = jnp.where(at, 0.0, full_i) - (fac_r * row_i + fac_i * row_r)
        return jnp.where(sub_col == j, pivot, pivots)

    pivots = lax.fori_loop(0, size, eliminate, jnp.ones((size, 1), F32))
    scale = math.sqrt(nodes) / jnp.sqrt(pivots)
    low = lane < sub
    inv_r = jnp.where(low, work_r[...], jnp.where(lane == sub, 1.0, 0.0)) * scale
    inv_i = jnp.where(low, work_i[...], 0.0) * scale
    turned = jnp.concatenate(
        [jnp.concatenate([inv_r, -inv_i], 1), jnp.concatenate([inv_i, inv_r], 1)], 0
    )
    out[...] = lax.dot_general(
        image[...], turned, (((1,), (1,)), ((), ())), precision=HIGH, preferred_element_type=F32
    )


def whitened(gram, image, nodes):
    size = image.shape[1] // 2
    vmem = pl.BlockSpec(memory_space=pltpu.VMEM)
    return pl.pallas_call(
        functools.partial(whiten_kernel, nodes),
        out_shape=jax.ShapeDtypeStruct(image.shape, F32),
        in_specs=[vmem, vmem],
        out_specs=vmem,
        scratch_shapes=[pltpu.VMEM((size, size), F32)] * 2,
    )(gram, image)


def on_device(response_tiles, tile_rows, tile_cols, tile_counts, start_block):
    slots = response_tiles[0, 0]
    shard, width = start_block.shape
    columns = width // 2
    tile = slots.shape[-1]
    own = shard * lax.axis_size("tiles")
    blocks = own // tile
    nodes = own * lax.axis_size("rows")
    first_block = lax.axis_index("rows") * blocks - blocks
    live = jnp.arange(slots.shape[0], dtype=jnp.int32) < tile_counts[0, 0]
    row = jnp.clip(tile_rows[0, 0], 0, blocks - 1)
    col = jnp.clip(tile_cols[0, 0] - first_block, 0, 3 * blocks - 1)
    dead = 4 * blocks
    plan = jnp.concatenate(
        [
            ordered(jnp.where(live, row, dead), col, blocks),
            ordered(jnp.where(live, col, dead), row, 3 * blocks),
        ]
    )
    current = start_block.astype(F32)
    image, gram = step(plan, slots, current, False)
    current = whitened(gram, image, nodes)
    image, gram = step(plan, slots, current, True)
    rayleigh = gram[columns:].reshape(columns, 2, columns).swapaxes(0, 1) / nodes
    current = whitened(gram, image, nodes)
    return (current, rayleigh)


def solution(mesh):
    in_specs = (
        P("rows", "tiles", None, None, None, None),
        P("rows", "tiles", None),
        P("rows", "tiles", None),
        P("rows", "tiles"),
        P(("rows", "tiles"), None),
    )
    out_specs = (P(("rows", "tiles"), None), P())
    return jax.shard_map(
        on_device, mesh=mesh, in_specs=in_specs, out_specs=out_specs, check_vma=False
    )
```

```python
import functools
import math

import jax
import jax.numpy as jnp
from jax import lax
from jax.experimental import pallas as pl
from jax.experimental.pallas import tpu as pltpu
from jax.sharding import PartitionSpec as P

HIGH = lax.Precision.HIGHEST
MESH = pl.DeviceIdType.MESH
VMEM_BYTES = 48 * 1024 * 1024
F32 = jnp.float32
BF16 = jnp.bfloat16
ITERS = 2


def ordered(key, other, outs):
    count = key.shape[0]
    slot = jnp.arange(count, dtype=jnp.int32)
    before = (key[:, None] < key[None, :]) | (
        (key[:, None] == key[None, :]) & (slot[:, None] < slot[None, :])
    )
    rank = jnp.sum(before.astype(jnp.int32), 0)
    hot = (rank[:, None] == slot[None, :]).astype(jnp.int32)
    order = jnp.sum(hot * slot[:, None], 0)
    target = jnp.sum(hot * key[:, None], 0)
    source = jnp.sum(hot * other[:, None], 0)
    same = jnp.concatenate([jnp.zeros((1,), bool), target[1:] == target[:-1]])
    previous = jnp.where(same, slot, 0)
    out = jnp.arange(outs, dtype=jnp.int32)
    upto = jnp.sum((target[:, None] <= out[None, :]).astype(jnp.int32), 0)
    present = jnp.any(target[:, None] == out[None, :], 0)
    return jnp.concatenate([order, source, previous, jnp.where(present, upto, 0)])


def whitening(gram, work_r, work_i, nodes):
    size = work_r.shape[0]
    work_r[...] = gram[:, 0:size]
    work_i[...] = -gram[:, size : 2 * size]
    lane = lax.broadcasted_iota(jnp.int32, (size, size), 1)
    sub = lax.broadcasted_iota(jnp.int32, (size, size), 0)
    lane_row = lax.broadcasted_iota(jnp.int32, (1, size), 1)
    sub_col = lax.broadcasted_iota(jnp.int32, (size, 1), 0)

    def eliminate(j, pivots):
        full_r, full_i = work_r[...], work_i[...]
        at = lane == j
        col_r = jnp.sum(jnp.where(at, full_r, 0.0), 1, keepdims=True)
        col_i = jnp.sum(jnp.where(at, full_i, 0.0), 1, keepdims=True)
        row_r = work_r[pl.ds(j, 1), :]
        row_i = work_i[pl.ds(j, 1), :]
        here = lane_row == j
        pivot = jnp.sum(jnp.where(here, row_r, 0.0), 1, keepdims=True)
        inverse = 1.0 / pivot
        below = sub_col > j
        fac_r = jnp.where(below, col_r * inverse, 0.0)
        fac_i = jnp.where(below, col_i * inverse, 0.0)
        row_r = jnp.where(here, 1.0, row_r)
        row_i = jnp.where(here, 0.0, row_i)
        work_r[...] = jnp.where(at, 0.0, full_r) - (fac_r * row_r - fac_i * row_i)
        work_i[...] = jnp.where(at, 0.0, full_i) - (fac_r * row_i + fac_i * row_r)
        return jnp.where(sub_col == j, pivot, pivots)

    pivots = lax.fori_loop(0, size, eliminate, jnp.ones((size, 1), F32))
    scale = math.sqrt(nodes) / jnp.sqrt(pivots)
    low = lane < sub
    inv_r = jnp.where(low, work_r[...], jnp.where(lane == sub, 1.0, 0.0)) * scale
    inv_i = jnp.where(low, work_i[...], 0.0) * scale
    return jnp.concatenate(
        [jnp.concatenate([inv_r, -inv_i], 1), jnp.concatenate([inv_i, inv_r], 1)], 0
    )


def kernel(
    n_g, n_t, slots_n, blocks,
    plan, tiles, start, subspace_out, rayleigh_out,
    turned, cur, ext, wide, ext_blocks, z_blocks, runs, part, rs_in, z_own, z_in, z_rows,
    spread, mid, halo_in, ar_out, ar_in,
    gram_mine, gram_in, gram_rows, gram_sum, work_r, work_i, white,
    gz_s, gz_r, gh_s, gh_r, rs_s, rs_r, ag_s, ag_r, ah_s, ah_r, ar_s, ar_r,
    g1_s, g1_r, g2_s, g2_r, g3_s, g3_r,
):
    g = lax.axis_index("rows")
    t = lax.axis_index("tiles")
    has_low = g > 0
    has_high = g < n_g - 1
    tile = tiles.shape[-1]
    shard, width = start.shape
    half = width // 2
    own = shard * n_t
    nodes = own * n_g
    base = 3 * slots_n + blocks

    barrier = pltpu.get_barrier_semaphore()
    for k in range(1, n_t):
        pl.semaphore_signal(barrier, inc=1, device_id=(g, (t + k) % n_t), device_id_type=MESH)

    for k in range(1, n_g):
        pl.semaphore_signal(barrier, inc=1, device_id=((g + k) % n_g, t), device_id_type=MESH)
    pl.semaphore_wait(barrier, n_t + n_g - 2)

    def remote(src, dst, send, recv, dev):
        return pltpu.make_async_remote_copy(
            src_ref=src, dst_ref=dst, send_sem=send, recv_sem=recv,
            device_id=dev, device_id_type=MESH,
        )

    def shard_at(base, index):
        return pl.ds(pl.multiple_of(base + index * shard, 64), shard)

    def both(do_up, do_down):
        pl.when(has_high)(do_up)
        pl.when(has_low)(do_down)

    def cross(left, right):
        full = lax.dot_general(
            left, right, (((0,), (0,)), ((), ())), precision=HIGH, preferred_element_type=F32
        )
        return jnp.concatenate(
            [full[:half, :half] + full[half:, half:], full[:half, half:] - full[half:, :half]], 1
        )

    def gathering(it, buf):
        def along(k, landed):
            at = buf.at[shard_at(own, (t - k + n_t) % n_t if landed else t)]
            return remote(at, at, gz_s.at[it, k], gz_r.at[it, k], (g, (t + k) % n_t))

        def halo(k, up):
            index = (t - k + n_t) % n_t
            side = 0 if up else 1
            return remote(
                buf.at[shard_at(own, index)],
                buf.at[shard_at(0 if up else 2 * own, index)],
                gh_s.at[it, side, k], gh_r.at[it, side, k],
                (g + 1 if up else g - 1, t),
            )

        def landed_halo(k, low):
            index = (t - k + n_t) % n_t
            side = 0 if low else 1
            at = buf.at[shard_at(0 if low else 2 * own, index)]
            return remote(
                at, at, gh_s.at[it, side, k], gh_r.at[it, side, k],
                (g - 1 if low else g + 1, t),
            )

        def begin(rows):
            buf[shard_at(own, t), :] = rows
            for k in range(1, n_t):
                along(k, False).start()
            both(lambda: halo(0, True).start(), lambda: halo(0, False).start())

        def forward_halo():
            for k in range(1, n_t):
                along(k, True).wait_recv()
                both(lambda k=k: halo(k, True).start(), lambda k=k: halo(k, False).start())

        def finish():
            for k in range(n_t):
                both(
                    lambda k=k: landed_halo(k, False).wait_recv(),
                    lambda k=k: landed_halo(k, True).wait_recv(),
                )
            for k in range(1, n_t):
                along(k, False).wait_send()
            for k in range(n_t):
                both(lambda k=k: halo(k, True).wait_send(), lambda k=k: halo(k, False).wait_send())

        return begin, forward_halo, finish

    cur[...] = start[...].astype(F32)
    begin, forward_halo, finish = gathering(0, ext)
    begin(start[...])

    @pl.when(jnp.logical_not(has_low))
    def _():
        ext[0:own, :] = jnp.zeros((own, width), BF16)
        wide[0:own, :] = jnp.zeros((own, width), F32)
        for it in range(ITERS):
            halo_in[it, 0] = jnp.zeros((own, width), BF16)

    @pl.when(jnp.logical_not(has_high))
    def _():
        ext[2 * own : 3 * own, :] = jnp.zeros((own, width), BF16)
        wide[2 * own : 3 * own, :] = jnp.zeros((own, width), F32)
        for it in range(ITERS):
            halo_in[it, 1] = jnp.zeros((own, width), BF16)

    runs[0] = jnp.zeros((tile, width), F32)
    forward_halo()

    def turn(s, _):
        for c in range(2):
            turned[s, pl.ds(c * tile, tile), :] = tiles[s, c].T
        return 0

    lax.fori_loop(0, slots_n, turn, 0)
    finish()
    for c in range(3 * blocks):
        ext_blocks[c] = ext[pl.ds(c * tile, tile), :]

    for it in range(ITERS):
        last = it == ITERS - 1

        def forward(s, _):
            pair = tiles[plan[s]].reshape(2 * tile, tile)
            both_terms = jnp.dot(pair, ext_blocks[plan[slots_n + s]], preferred_element_type=F32)
            re, im = both_terms[:tile], both_terms[tile:]
            term = jnp.concatenate(
                [re[:, :half] - im[:, half:], re[:, half:] + im[:, :half]], 1
            )
            runs[s + 1] = term + runs[plan[2 * slots_n + s]]
            return 0

        lax.fori_loop(0, slots_n, forward, 0)
        for r in range(blocks):
            part[pl.ds(r * tile, tile), :] = runs[plan[3 * slots_n + r]]

        def reduce_z(k):
            dest = (t + k) % n_t
            return remote(
                part.at[shard_at(0, dest)], rs_in.at[it, k], rs_s.at[it, k], rs_r.at[it, k], (g, dest)
            )

        for k in range(1, n_t):
            reduce_z(k).start()
        total = part[shard_at(0, t), :]
        for k in range(1, n_t):
            reduce_z(k).wait_recv()
            total += rs_in[it, k]
        z_own[...] = total.astype(BF16)

        def spread_z(k):
            return remote(z_own, z_in.at[it, k], ag_s.at[it, k], ag_r.at[it, k], (g, (t + k) % n_t))

        for k in range(1, n_t):
            spread_z(k).start()
        z_rows[shard_at(0, t), :] = z_own[...]
        for k in range(1, n_t):
            spread_z(k).wait_recv()
            z_rows[shard_at(0, (t - k + n_t) % n_t), :] = z_in[it, k]
        for r in range(blocks):
            z_blocks[r] = z_rows[pl.ds(r * tile, tile), :]

        def adjoint(s, _):
            source = z_blocks[plan[base + slots_n + s]]
            both_terms = jnp.dot(turned[plan[base + s]], source, preferred_element_type=F32)
            re, im = both_terms[:tile], both_terms[tile:]
            term = jnp.concatenate(
                [re[:, :half] + im[:, half:], re[:, half:] - im[:, :half]], 1
            )
            runs[s + 1] = term + runs[plan[base + 2 * slots_n + s]]
            return 0

        lax.fori_loop(0, slots_n, adjoint, 0)
        for c in list(range(blocks)) + list(range(2 * blocks, 3 * blocks)):
            spread[pl.ds(c * tile, tile), :] = runs[plan[base + 3 * slots_n + c]].astype(BF16)

        def rim(k, up):
            dest = (t + k) % n_t
            side = 0 if up else 1
            return remote(
                spread.at[shard_at(2 * own if up else 0, dest)],
                halo_in.at[it, side, shard_at(0, dest)],
                ah_s.at[it, side, k], ah_r.at[it, side, k],
                (g + 1 if up else g - 1, t),
            )

        for k in list(range(1, n_t)) + [0]:
            both(lambda k=k: rim(k, True).start(), lambda k=k: rim(k, False).start())
        for c in range(blocks):
            mid[pl.ds(c * tile, tile), :] = runs[plan[base + 3 * slots_n + blocks + c]]

        def sum_to(k):
            return remote(
                ar_out.at[k], ar_in.at[it, k], ar_s.at[it, k], ar_r.at[it, k], (g, (t + k) % n_t)
            )

        for k in list(range(1, n_t)) + [0]:
            both(lambda k=k: rim(k, False).wait_recv(), lambda k=k: rim(k, True).wait_recv())
            at = shard_at(0, (t + k) % n_t)
            total = mid[at, :] + halo_in[it, 0, at, :].astype(F32) + halo_in[it, 1, at, :].astype(F32)
            if k:
                ar_out[k] = total.astype(BF16)
                sum_to(k).start()
        for k in range(1, n_t):
            sum_to(k).wait_recv()
            total += ar_in[it, k].astype(F32)
        image = total + cur[...]
        if not last:
            begin, forward_halo, finish = gathering(1, wide)
            begin(image)

        gram_mine[it, 0:half, :] = cross(image, image)
        if last:
            gram_mine[it, half : 2 * half, :] = cross(cur[...], image)
        cur[...] = image
        piece = (2 * half if last else half) // n_t

        def piece_at(index):
            return pl.ds(pl.multiple_of(index * piece, 8), piece)

        def gram_one(k):
            dest = (t + k) % n_t
            return remote(
                gram_mine.at[it, piece_at(dest)], gram_in.at[it, k, pl.ds(0, piece)],
                g1_s.at[it, k], g1_r.at[it, k], (g, dest),
            )

        for k in range(1, n_t):
            gram_one(k).start()
        total = gram_mine[it, piece_at(t), :]
        for k in range(1, n_t):
            gram_one(k).wait_recv()
            total += gram_in[it, k, 0:piece, :]
        gram_rows[it, g, 0:piece, :] = total

        def gram_two(k, landed):
            at = gram_rows.at[it, (g - k + n_g) % n_g if landed else g, pl.ds(0, piece)]
            return remote(at, at, g2_s.at[it, k], g2_r.at[it, k], ((g + k) % n_g, t))

        for k in range(1, n_g):
            gram_two(k, False).start()
        for k in range(1, n_g):
            gram_two(k, True).wait_recv()
        total = gram_rows[it, 0, 0:piece, :]
        for k in range(1, n_g):
            total += gram_rows[it, k, 0:piece, :]
        gram_sum[it, piece_at(t), :] = total

        def gram_three(k, landed):
            at = gram_sum.at[it, piece_at((t - k + n_t) % n_t if landed else t)]
            return remote(at, at, g3_s.at[it, k], g3_r.at[it, k], (g, (t + k) % n_t))

        for k in range(1, n_t):
            gram_three(k, False).start()
        for k in range(1, n_t):
            gram_three(k, True).wait_recv()

        for k in range(1, n_t):
            reduce_z(k).wait_send()
            spread_z(k).wait_send()
            sum_to(k).wait_send()
            gram_one(k).wait_send()
            gram_three(k, False).wait_send()
        for k in range(n_t):
            both(lambda k=k: rim(k, True).wait_send(), lambda k=k: rim(k, False).wait_send())
        for k in range(1, n_g):
            gram_two(k, False).wait_send()

        if not last:
            forward_halo()
        white[...] = whitening(gram_sum[it, 0:half, :], work_r, work_i, nodes).T

        def times_white(rows):
            return jnp.dot(rows, white[...], precision=HIGH, preferred_element_type=F32)

        if last:
            subspace_out[...] = times_white(cur[...])
            products = gram_sum[it, half : 2 * half, :]
            rayleigh_out[0] = products[:, :half] / nodes
            rayleigh_out[1] = products[:, half:] / nodes
        else:
            cur[...] = times_white(cur[...])
            finish()

            def narrow(c, _):
                rows = wide[pl.ds(pl.multiple_of(c * tile, tile), tile), :]
                ext_blocks[c] = times_white(rows).astype(BF16)
                return 0

            lax.fori_loop(0, 3 * blocks, narrow, 0)


def iterate(plan, tiles, start):
    n_g, n_t = lax.axis_size("rows"), lax.axis_size("tiles")
    slots_n, _, tile, _ = tiles.shape
    shard, width = start.shape
    half = width // 2
    own = shard * n_t
    blocks = own // tile
    vmem = pl.BlockSpec(memory_space=pltpu.VMEM)
    along = pltpu.SemaphoreType.DMA((ITERS, n_t))
    sides = pltpu.SemaphoreType.DMA((ITERS, 2, n_t))
    groups = pltpu.SemaphoreType.DMA((ITERS, n_g))
    scratch = [
        ((slots_n, 2 * tile, tile), BF16),
        ((shard, width), F32),
        ((3 * own, width), BF16),
        ((3 * own, width), F32),
        ((3 * blocks, tile, width), BF16),
        ((blocks, tile, width), BF16),
        ((slots_n + 1, tile, width), F32),
        ((own, width), F32),
        ((ITERS, n_t, shard, width), F32),
        ((shard, width), BF16),
        ((ITERS, n_t, shard, width), BF16),
        ((own, width), BF16),
        ((3 * own, width), BF16),
        ((own, width), F32),
        ((ITERS, 2, own, width), BF16),
        ((n_t, shard, width), BF16),
        ((ITERS, n_t, shard, width), BF16),
        ((ITERS, width, width), F32),
        ((ITERS, n_t, width // n_t, width), F32),
        ((ITERS, n_g, width // n_t, width), F32),
        ((ITERS, width, width), F32),
        ((half, half), F32),
        ((half, half), F32),
        ((width, width), F32),
    ]
    return pl.pallas_call(
        functools.partial(kernel, n_g, n_t, slots_n, blocks),
        out_shape=(
            jax.ShapeDtypeStruct((shard, width), F32),
            jax.ShapeDtypeStruct((2, half, half), F32),
        ),
        in_specs=[pl.BlockSpec(memory_space=pltpu.SMEM), vmem, vmem],
        out_specs=(vmem, vmem),
        scratch_shapes=[pltpu.VMEM(shape, dtype) for shape, dtype in scratch]
        + [along, along, sides, sides, along, along, along, along, sides, sides, along, along]
        + [along, along, groups, groups, along, along],
        compiler_params=pltpu.CompilerParams(
            collective_id=0, has_side_effects=True, vmem_limit_bytes=VMEM_BYTES
        ),
    )(plan, tiles, start)


def on_device(response_tiles, tile_rows, tile_cols, tile_counts, start_block):
    slots = response_tiles[0, 0]
    shard = start_block.shape[0]
    tile = slots.shape[-1]
    own = shard * lax.axis_size("tiles")
    blocks = own // tile
    first_block = lax.axis_index("rows") * blocks - blocks
    live = jnp.arange(slots.shape[0], dtype=jnp.int32) < tile_counts[0, 0]
    row = jnp.clip(tile_rows[0, 0], 0, blocks - 1)
    col = jnp.clip(tile_cols[0, 0] - first_block, 0, 3 * blocks - 1)
    dead = 4 * blocks
    plan = jnp.concatenate(
        [
            ordered(jnp.where(live, row, dead), col, blocks),
            ordered(jnp.where(live, col, dead), row, 3 * blocks),
        ]
    )
    return iterate(plan, slots, start_block)


def solution(mesh):
    in_specs = (
        P("rows", "tiles", None, None, None, None),
        P("rows", "tiles", None),
        P("rows", "tiles", None),
        P("rows", "tiles"),
        P(("rows", "tiles"), None),
    )
    out_specs = (P(("rows", "tiles"), None), P())
    return jax.shard_map(
        on_device, mesh=mesh, in_specs=in_specs, out_specs=out_specs, check_vma=False
    )
```
